32 devices in a mesh: leaf: 32 (over z, y, x, core).
Axes of the slice: x: 2, y: 2, z: 4, core: 2. Of those that a mesh axis runs over, the one named last changes fastest.
Arguments:
- charges: bfloat16 [8192, 128, 128], P('leaf'), may hold values from -6 to 6
- basis_in: bfloat16 [8192, 64, 128], P('leaf'), may hold values from -0.5 to 0.5
- basis_out: bfloat16 [8192, 64, 128], P('leaf'), may hold values from -0.75 to 0.75
- transfer: bfloat16 [1024, 8, 64, 64], P('leaf'), may hold values from -0.375 to 0.375
- leaf_coupling: bfloat16 [16, 64, 64], replicated, may hold values from -0.25 to 0.25
- parent_coupling: bfloat16 [16, 64, 64], replicated, may hold values from -0.25 to 0.25
- leaf_sources: int32 [8192, 16], P('leaf'), may hold values from 0 to 511, as said below
- leaf_counts: int32 [8192], P('leaf'), may hold values from 2 to 16
- leaf_sends: int32 [32, 2, 128], replicated, may hold values from 0 to 255, as said below
- parent_sources: int32 [1024, 16], P('leaf'), may hold values from 0 to 63, as said below
- parent_counts: int32 [1024], P('leaf'), may hold values from 12 to 16
- parent_sends: int32 [32, 32], replicated, may hold values from 0 to 31
Outputs:
- potential: bfloat16 [8192, 128, 128], P('leaf')
The draws below stay inside these ranges and needn't reach their ends.
Inputs may be any that keep to these rules, and one draw needn't show every extreme that they name: `leaf_sources`: every row of a device's leaf pool is read by some used slot of that device's leaf lists. `leaf_sends`: the 128 leaves offered in one direction are distinct. `parent_sources`: every row of a device's parent pool is read by some used slot of that device's parent lists.
All inputs are finite; a program needn't handle non-finite values.
Results may differ from the reference program's by a relative error of at most 0.007.
Values may be sent and summed in bfloat16 or wider, within the bound.
A program may use at most 256 MiB of HBM per device.

```python
import jax
import jax.numpy as jnp
from jax import lax

K = 64
R = 128
PTS = 128
LIST0 = 16
LIST1 = 16
LEAF_DEV = 256
NODE1 = 32
SIDE = 128
LEAVES = 8192
NODES1 = 1024
N_LEAF = 32


def pool_columns(device_key, pool_size, targets, list_width):
    leading_cols = -(-pool_size // targets)
    spare = leading_cols * targets - pool_size
    order = jax.random.permutation(jax.random.fold_in(device_key, 1), pool_size).astype(jnp.int32)
    filler = jax.random.randint(jax.random.fold_in(device_key, 2), (spare,), 0, pool_size, dtype=jnp.int32)
    leading = jnp.concatenate([order, filler]).reshape(leading_cols, targets).T
    trailing = jax.random.randint(jax.random.fold_in(device_key, 3), (targets, list_width - leading_cols), 0, pool_size, dtype=jnp.int32)
    return jnp.concatenate([leading, trailing], 1)


def draw_leaf_sources(key, part):
    key = jax.random.fold_in(key, 11)

    def one_device(device_key):
        return pool_columns(device_key, LEAF_DEV + 2 * SIDE, LEAF_DEV, LIST0)
    return jax.vmap(one_device)(jax.random.split(key, N_LEAF)).reshape(LEAVES, LIST0)


def draw_parent_sources(key, part):
    key = jax.random.fold_in(key, 14)

    def one_device(device_key):
        return pool_columns(device_key, NODE1 + N_LEAF, NODE1, LIST1)
    return jax.vmap(one_device)(jax.random.split(key, N_LEAF)).reshape(NODES1, LIST1)


def draw_leaf_counts(key, part):
    key = jax.random.fold_in(key, 12)
    tops = jax.random.randint(jax.random.fold_in(key, 1), (N_LEAF, 1), LIST0 // 2, LIST0 + 1, dtype=jnp.int32)
    first = jax.random.randint(jax.random.fold_in(key, 2), (N_LEAF, LEAF_DEV), 0, 1 << 20, dtype=jnp.int32) % (tops - 1)
    second = jax.random.randint(jax.random.fold_in(key, 3), (N_LEAF, LEAF_DEV), 0, 1 << 20, dtype=jnp.int32) % (tops - 1)
    counts = (2 + jnp.maximum(first, second)).reshape(LEAVES)
    chosen = jax.random.randint(jax.random.fold_in(key, 4), (), 0, LEAVES, dtype=jnp.int32)
    positions = jnp.arange(LEAVES, dtype=jnp.int32)
    counts = jnp.where(positions == chosen, LIST0, counts)
    counts = jnp.where(positions == (chosen + 1) % LEAVES, 2, counts)
    return counts.astype(jnp.int32)


def draw_parent_counts(key, part):
    key = jax.random.fold_in(key, 15)
    counts = jax.random.randint(jax.random.fold_in(key, 1), (NODES1,), LIST1 - LIST1 // 4, LIST1 + 1, dtype=jnp.int32)
    chosen = jax.random.randint(jax.random.fold_in(key, 2), (), 0, NODES1, dtype=jnp.int32)
    positions = jnp.arange(NODES1, dtype=jnp.int32)
    counts = jnp.where(positions == chosen, LIST1, counts)
    counts = jnp.where(positions == (chosen + 1) % NODES1, LIST1 - LIST1 // 4, counts)
    return counts.astype(jnp.int32)


def draw_leaf_sends(key, part):
    key = jax.random.fold_in(key, 13)

    def one_row(row_key):
        return jax.random.permutation(row_key, LEAF_DEV)[:SIDE].astype(jnp.int32)
    return jax.vmap(one_row)(jax.random.split(key, 2 * N_LEAF)).reshape(N_LEAF, 2, SIDE)


def draw_parent_sends(key, part):
    key = jax.random.fold_in(key, 16)
    return jax.random.randint(key, (N_LEAF, N_LEAF), 0, NODE1, dtype=jnp.int32)


def block_scale(rng, extent, cuts, least, high):
    def one(axis_at, shards_of):
        draws = jax.random.uniform(jax.random.fold_in(jax.random.fold_in(rng, 6), axis_at), (shards_of,), jnp.float32, least / len(cuts), high / len(cuts))
        return jnp.repeat(jnp.exp(draws), extent[axis_at] // shards_of).reshape((-1,) + (1,) * (len(extent) - axis_at - 1))

    factor_of = one(*cuts[0])
    for cut in cuts[1:]:
        factor_of = factor_of * one(*cut)
    return factor_of


def noise(own_key, dims, width, limit, cuts=(), kind=jnp.bfloat16):
    gain = block_scale(own_key, dims, cuts, -0.22, 0.18) if cuts else 1.0
    values = jax.random.normal(own_key, dims, jnp.float32) * width * gain
    return jnp.minimum(jnp.maximum(values, -limit), limit).astype(kind)


def setup_inputs(seed: int = 0) -> dict:
    key_list = jax.random.split(jax.random.key(seed), 13)
    return {
        "charges": noise(key_list[0], (LEAVES, PTS, R), 1.0, 6.0, ((0, 32),)),
        "basis_in": noise(key_list[1], (LEAVES, K, PTS), PTS ** -0.5, 0.5, ((0, 32),)),
        "basis_out": noise(key_list[2], (LEAVES, K, PTS), K ** -0.5, 0.75, ((0, 32),)),
        "transfer": noise(key_list[3], (NODES1, 8, K, K), (4 * K) ** -0.5, 0.375, ((0, 32),)),
        "leaf_coupling": noise(key_list[4], (LIST0, K, K), (K * LIST0 // 2) ** -0.5, 0.25),
        "parent_coupling": noise(key_list[5], (LIST1, K, K), (K * LIST1 // 2) ** -0.5, 0.25),
        "leaf_sources": draw_leaf_sources(jax.random.fold_in(key_list[12], 71), 0),
        "leaf_counts": draw_leaf_counts(jax.random.fold_in(key_list[12], 71), 0),
        "leaf_sends": draw_leaf_sends(jax.random.fold_in(key_list[12], 71), 0),
        "parent_sources": draw_parent_sources(jax.random.fold_in(key_list[12], 71), 0),
        "parent_counts": draw_parent_counts(jax.random.fold_in(key_list[12], 71), 0),
        "parent_sends": draw_parent_sends(jax.random.fold_in(key_list[12], 71), 0),
    }


def split_devices(array):
    return array.reshape((N_LEAF, array.shape[0] // N_LEAF) + array.shape[1:])


def pooled_product(pool_rows, sources, counts, coupling):
    list_width = sources.shape[1]
    valid_mask = jnp.arange(list_width, dtype=jnp.int32)[None, :] < counts[:, None]
    picked = jnp.where(valid_mask[:, :, None, None], pool_rows[sources], jnp.zeros((), pool_rows.dtype))
    return jnp.einsum("jab,tjbr->tar", coupling.astype(jnp.float32), picked.astype(jnp.float32))


def reference(charges, basis_in, basis_out, transfer, leaf_coupling, parent_coupling, leaf_sources, leaf_counts, leaf_sends, parent_sources, parent_counts, parent_sends):
    def upward(pieces):
        densities, columns, parents = pieces
        leaf_up = jnp.einsum("nkp,npr->nkr", columns.astype(jnp.float32), densities.astype(jnp.float32)).astype(jnp.bfloat16)
        leaf_up = lax.optimization_barrier(leaf_up)
        grouped = leaf_up.astype(jnp.float32).reshape(NODE1, 8, K, R)
        parent_up = jnp.einsum("pcab,pcar->pbr", parents.astype(jnp.float32), grouped).astype(jnp.bfloat16)
        return leaf_up, parent_up

    up_leaf, up_parent = lax.map(upward, (split_devices(charges), split_devices(basis_in), split_devices(transfer)))
    sources_leaf = split_devices(leaf_sources)
    counts_leaf = split_devices(leaf_counts)
    sources_parent = split_devices(parent_sources)
    counts_parent = split_devices(parent_counts)
    rows_out = split_devices(basis_out)
    transfers = split_devices(transfer)
    device_ids = jnp.arange(N_LEAF, dtype=jnp.int32)

    def per_device(device):
        left_dev = jnp.maximum(device - 1, 0)
        right_dev = jnp.minimum(device + 1, N_LEAF - 1)
        from_left = up_leaf[left_dev][leaf_sends[left_dev, 1]]
        from_left = jnp.where(device > 0, from_left, jnp.zeros_like(from_left))
        from_right = up_leaf[right_dev][leaf_sends[right_dev, 0]]
        from_right = jnp.where(device < N_LEAF - 1, from_right, jnp.zeros_like(from_right))
        leaf_pool = jnp.concatenate([up_leaf[device], from_left, from_right], 0)
        leaf_field = pooled_product(leaf_pool, sources_leaf[device], counts_leaf[device], leaf_coupling)
        arrived = up_parent[device_ids, parent_sends[:, device]]
        parent_pool = jnp.concatenate([up_parent[device], arrived], 0)
        parent_field = pooled_product(parent_pool, sources_parent[device], counts_parent[device], parent_coupling)
        parent_down = lax.optimization_barrier(parent_field.astype(jnp.bfloat16))
        pushed = jnp.einsum("pcab,pbr->pcar", transfers[device].astype(jnp.float32), parent_down.astype(jnp.float32)).reshape(LEAF_DEV, K, R)
        leaf_total = lax.optimization_barrier((leaf_field + pushed).astype(jnp.bfloat16))
        return jnp.einsum("nkp,nkr->npr", rows_out[device].astype(jnp.float32), leaf_total.astype(jnp.float32)).astype(jnp.bfloat16)

    return lax.map(per_device, device_ids).reshape(LEAVES, PTS, R)
```

```python
import functools

import jax
import jax.numpy as jnp
from jax import lax
from jax.experimental import pallas as pl
from jax.experimental.pallas import tpu as pltpu
from jax.sharding import PartitionSpec as P

CHUNKS = 4
ANY = pl.BlockSpec(memory_space=pl.ANY)
SMEM = pl.BlockSpec(memory_space=pltpu.SMEM)
CONTRACT_FIRST = (((0,), (0,)), ((), ()))


def upward_kernel(
    n,
    steps,
    charges,
    basis_in,
    transfer,
    leaf_sends,
    parent_sends,
    up_out,
    remote_out,
    parents_out,
    up_all,
    parent_all,
    stage,
    parent_stage,
    zeros,
    send_sem,
    recv_sem,
    parent_send_sem,
    parent_recv_sem,
    local_sem,
):
    me = lax.axis_index("leaf")
    step = pl.program_id(0)
    block = charges.shape[0]
    parents = transfer.shape[0]
    rank, rhs = up_all.shape[1:]
    own_parents = parent_all.shape[0]
    side = stage.shape[1]
    piece = side // CHUNKS

    @pl.when(step == 0)
    def _():
        barrier = pltpu.get_barrier_semaphore()

        def greet(k, carry):
            pl.semaphore_signal(
                barrier,
                inc=1,
                device_id=(lax.rem(me + k, n),),
                device_id_type=pl.DeviceIdType.MESH,
            )
            return carry

        lax.fori_loop(1, n, greet, 0)

    for leaf in range(block):
        row = jnp.dot(basis_in[leaf], charges[leaf], preferred_element_type=jnp.float32).astype(jnp.bfloat16)
        up_out[leaf] = row
        up_all[step * block + leaf] = row
    for p in range(parents):
        children = up_out[8 * p : 8 * p + 8].reshape(8 * rank, rhs)
        parent_all[step * parents + p] = lax.dot_general(
            transfer[p].reshape(8 * rank, rank), children, CONTRACT_FIRST, preferred_element_type=jnp.float32
        ).astype(jnp.bfloat16)

    @pl.when(step == steps - 1)
    def _():
        pl.semaphore_wait(pltpu.get_barrier_semaphore(), n - 1)

        def leaf_copy(direction, c):
            target = me - 1 if direction == 0 else me + 1
            return pltpu.make_async_remote_copy(
                src_ref=stage.at[direction, pl.ds(c * piece, piece)],
                dst_ref=remote_out.at[pl.ds((1 - direction) * side + c * piece, piece)],
                send_sem=send_sem.at[direction, c],
                recv_sem=recv_sem.at[direction, c],
                device_id=(target,),
                device_id_type=pl.DeviceIdType.MESH,
            )

        def zero_copy(half, c):
            return pltpu.make_async_copy(
                zeros, remote_out.at[pl.ds(half * side + c * piece, piece)], local_sem.at[1 + half, c]
            )

        def has_target(direction):
            return me > 0 if direction == 0 else me < n - 1

        for c in range(CHUNKS):
            for direction in range(2):

                def fill(i, carry):
                    stage[direction, c * piece + i] = up_all[leaf_sends[me, direction, c * piece + i]]
                    return carry

                lax.fori_loop(0, piece, fill, 0, unroll=4)

                @pl.when(has_target(direction))
                def _():
                    leaf_copy(direction, c).start()

        def fill_parent(d, carry):
            parent_stage[d] = parent_all[parent_sends[me, d]]
            return carry

        lax.fori_loop(0, n, fill_parent, 0)

        def parent_copy(k):
            target = lax.rem(me + k, n)
            return pltpu.make_async_remote_copy(
                src_ref=parent_stage.at[target],
                dst_ref=parents_out.at[own_parents + me],
                send_sem=parent_send_sem.at[k],
                recv_sem=parent_recv_sem.at[k],
                device_id=(target,),
                device_id_type=pl.DeviceIdType.MESH,
            )

        def start_parent(k, carry):
            parent_copy(k).start()
            return carry

        lax.fori_loop(1, n, start_parent, 0)
        own = [
            pltpu.make_async_copy(parent_all, parents_out.at[pl.ds(0, own_parents)], local_sem.at[0, 0]),
            pltpu.make_async_copy(parent_stage.at[me], parents_out.at[own_parents + me], local_sem.at[0, 1]),
        ]
        for copy in own:
            copy.start()
        zeros[...] = jnp.zeros_like(zeros)
        for half in range(2):

            @pl.when(jnp.logical_not(has_target(half)))
            def _():
                for c in range(CHUNKS):
                    zero_copy(half, c).start()
                for c in range(CHUNKS):
                    zero_copy(half, c).wait()

        for copy in own:
            copy.wait()

        def wait_parent(k, carry):
            source = lax.rem(me - k + n, n)
            copy = pltpu.make_async_remote_copy(
                src_ref=parent_stage.at[lax.rem(me + k, n)],
                dst_ref=parents_out.at[own_parents + source],
                send_sem=parent_send_sem.at[k],
                recv_sem=parent_recv_sem.at[k],
                device_id=(lax.rem(me + k, n),),
                device_id_type=pl.DeviceIdType.MESH,
            )
            copy.wait_send()
            copy.wait_recv()
            return carry

        lax.fori_loop(1, n, wait_parent, 0)
        for c in range(CHUNKS):
            for direction in range(2):

                @pl.when(has_target(direction))
                def _():
                    leaf_copy(direction, c).wait_send()

                @pl.when(has_target(1 - direction))
                def _():
                    leaf_copy(direction, c).wait_recv()


def field_pair(first, second, pool, sources, counts, stacked):
    width = sources.shape[1]
    spare = pool.shape[0] - 1
    columns = []
    for target in (first, second):
        limit = counts[target]
        rows = [pool[jnp.where(j < limit, sources[target, j], spare)] for j in range(width)]
        columns.append(jnp.concatenate(rows, 0))
    return jnp.dot(stacked[...], jnp.concatenate(columns, 1), preferred_element_type=jnp.float32)


def downward_kernel(
    leaf_sources,
    leaf_counts,
    parent_sources,
    parent_counts,
    leaf_coupling,
    parent_coupling,
    up_leaf,
    remote,
    parent_pool,
    transfer,
    basis_out,
    potential,
    pool,
    ppool,
    stacked,
    pstacked,
    down,
    sem,
):
    step = pl.program_id(0)
    block = basis_out.shape[0]
    parents = transfer.shape[0]
    own, rank, rhs = up_leaf.shape
    far = remote.shape[0]
    all_parents = parent_pool.shape[0]

    @pl.when(step == 0)
    def _():
        copies = [
            pltpu.make_async_copy(parent_pool, ppool.at[pl.ds(0, all_parents)], sem.at[0]),
            pltpu.make_async_copy(up_leaf, pool.at[pl.ds(0, own)], sem.at[1]),
            pltpu.make_async_copy(remote, pool.at[pl.ds(own, far)], sem.at[2]),
        ]
        for copy in copies:
            copy.start()
        pool[own + far] = jnp.zeros((rank, rhs), pool.dtype)
        ppool[all_parents] = jnp.zeros((rank, rhs), ppool.dtype)
        for j in range(leaf_coupling.shape[0]):
            stacked[:, j * rank : (j + 1) * rank] = leaf_coupling[j]
        for j in range(parent_coupling.shape[0]):
            pstacked[:, j * rank : (j + 1) * rank] = parent_coupling[j]
        copies[0].wait()

        def parent_pair(i, carry):
            field = field_pair(2 * i, 2 * i + 1, ppool, parent_sources, parent_counts, pstacked)
            down[2 * i] = field[:, :rhs].astype(down.dtype)
            down[2 * i + 1] = field[:, rhs:].astype(down.dtype)
            return carry

        lax.fori_loop(0, down.shape[0] // 2, parent_pair, 0)
        copies[1].wait()
        copies[2].wait()

    for p in range(parents):
        pushed = jnp.dot(
            transfer[p].reshape(8 * rank, rank), down[step * parents + p], preferred_element_type=jnp.float32
        )
        for c in range(0, 8, 2):
            leaf = 8 * p + c
            target = step * block + leaf
            field = field_pair(target, target + 1, pool, leaf_sources, leaf_counts, stacked)
            for k in range(2):
                total = field[:, k * rhs : (k + 1) * rhs] + pushed[(c + k) * rank : (c + k + 1) * rank]
                potential[leaf + k] = lax.dot_general(
                    basis_out[leaf + k],
                    total.astype(jnp.bfloat16),
                    CONTRACT_FIRST,
                    preferred_element_type=jnp.float32,
                ).astype(potential.dtype)


def shards(
    n,
    charges,
    basis_in,
    basis_out,
    transfer,
    leaf_coupling,
    parent_coupling,
    leaf_sources,
    leaf_counts,
    leaf_sends,
    parent_sources,
    parent_counts,
    parent_sends,
):
    leaves, points, rhs = charges.shape
    rank = basis_in.shape[1]
    parents = transfer.shape[0]
    side = leaf_sends.shape[2]
    per_step = 2
    steps = parents // per_step
    block = 8 * per_step
    bf16 = jnp.bfloat16
    up_leaf, remote, parent_pool = pl.pallas_call(
        functools.partial(upward_kernel, n, steps),
        grid=(steps,),
        out_shape=(
            jax.ShapeDtypeStruct((leaves, rank, rhs), bf16),
            jax.ShapeDtypeStruct((2 * side, rank, rhs), bf16),
            jax.ShapeDtypeStruct((parents + n, rank, rhs), bf16),
        ),
        in_specs=[
            pl.BlockSpec((block, points, rhs), lambda i: (i, 0, 0)),
            pl.BlockSpec((block, rank, points), lambda i: (i, 0, 0)),
            pl.BlockSpec((per_step, 8, rank, rank), lambda i: (i, 0, 0, 0)),
            SMEM,
            SMEM,
        ],
        out_specs=(pl.BlockSpec((block, rank, rhs), lambda i: (i, 0, 0)), ANY, ANY),
        scratch_shapes=[
            pltpu.VMEM((leaves, rank, rhs), bf16),
            pltpu.VMEM((parents, rank, rhs), bf16),
            pltpu.VMEM((2, side, rank, rhs), bf16),
            pltpu.VMEM((n, rank, rhs), bf16),
            pltpu.VMEM((side // CHUNKS, rank, rhs), bf16),
            pltpu.SemaphoreType.DMA((2, CHUNKS)),
            pltpu.SemaphoreType.DMA((2, CHUNKS)),
            pltpu.SemaphoreType.DMA((n,)),
            pltpu.SemaphoreType.DMA((n,)),
            pltpu.SemaphoreType.DMA((3, CHUNKS)),
        ],
        compiler_params=pltpu.CompilerParams(
            collective_id=0, has_side_effects=True, vmem_limit_bytes=40 * 2**20
        ),
        name="upward",
    )(charges, basis_in, transfer, leaf_sends, parent_sends)
    whole = lambda a: pl.BlockSpec(a.shape, lambda i, *_: (0,) * a.ndim)
    return pl.pallas_call(
        downward_kernel,
        out_shape=jax.ShapeDtypeStruct((leaves, points, rhs), bf16),
        grid_spec=pltpu.PrefetchScalarGridSpec(
            num_scalar_prefetch=4,
            grid=(steps,),
            in_specs=[
                whole(leaf_coupling),
                whole(parent_coupling),
                ANY,
                ANY,
                ANY,
                pl.BlockSpec((per_step, 8, rank, rank), lambda i, *_: (i, 0, 0, 0)),
                pl.BlockSpec((block, rank, points), lambda i, *_: (i, 0, 0)),
            ],
            out_specs=pl.BlockSpec((block, points, rhs), lambda i, *_: (i, 0, 0)),
            scratch_shapes=[
                pltpu.VMEM((leaves + 2 * side + 1, rank, rhs), bf16),
                pltpu.VMEM((parents + n + 1, rank, rhs), bf16),
                pltpu.VMEM((rank, leaf_sources.shape[1] * rank), bf16),
                pltpu.VMEM((rank, parent_sources.shape[1] * rank), bf16),
                pltpu.VMEM((parents, rank, rhs), bf16),
                pltpu.SemaphoreType.DMA((3,)),
            ],
        ),
        compiler_params=pltpu.CompilerParams(vmem_limit_bytes=40 * 2**20),
        name="downward",
    )(
        leaf_sources,
        leaf_counts,
        parent_sources,
        parent_counts,
        leaf_coupling,
        parent_coupling,
        up_leaf,
        remote,
        parent_pool,
        transfer,
        basis_out,
    )


def solution(mesh):
    return jax.shard_map(
        functools.partial(shards, mesh.shape["leaf"]),
        mesh=mesh,
        in_specs=(
            P("leaf", None, None),
            P("leaf", None, None),
            P("leaf", None, None),
            P("leaf", None, None, None),
            P(),
            P(),
            P("leaf", None),
            P("leaf"),
            P(),
            P("leaf", None),
            P("leaf"),
            P(),
        ),
        out_specs=P("leaf", None, None),
        check_vma=False,
    )
```

```python
import functools

import jax
import jax.numpy as jnp
from jax import lax
from jax.experimental import pallas as pl
from jax.experimental.pallas import tpu as pltpu
from jax.sharding import PartitionSpec as P

CHUNKS = 4
LOADS = 8
GROUP = 4
CODE = 1024
ANY = pl.BlockSpec(memory_space=pl.ANY)
SMEM = pl.BlockSpec(memory_space=pltpu.SMEM)
VMEM = pl.BlockSpec(memory_space=pltpu.VMEM)
CONTRACT_FIRST = (((0,), (0,)), ((), ()))
MESH = pl.DeviceIdType.MESH


def field_pair(first, second, pool, slots, stacked):
    columns = [
        jnp.concatenate([pool[slots[j, target]] for j in range(slots.shape[0])], 0) for target in (first, second)
    ]
    return jnp.dot(stacked[...], jnp.concatenate(columns, 1), preferred_element_type=jnp.float32)


def upward_kernel(
    n,
    charges_hbm,
    basis_hbm,
    transfer_hbm,
    leaf_sends,
    parent_sends,
    near_slots,
    parent_slots,
    far_codes,
    leaf_coupling,
    parent_coupling,
    far_out,
    field_out,
    list_out,
    charges,
    basis_in,
    transfer,
    up_all,
    near,
    far_stage,
    fast_stage,
    parent_all,
    parent_stage,
    parent_pool,
    down,
    field,
    stacked,
    pstacked,
    zeros,
    load_sem,
    far_sem,
    fast_sem,
    parent_send_sem,
    parent_recv_sem,
    zero_sem,
    field_sem,
):
    me = lax.axis_index("leaf")
    odd = lax.rem(me, 2)
    fast_target = me + 1 - 2 * odd
    far_target = me - 1 + 2 * odd
    has_far = jnp.logical_and(far_target >= 0, far_target < n)
    leaves, rank, rhs = up_all.shape
    parents = parent_all.shape[0]
    side = far_stage.shape[0]
    piece = side // CHUNKS
    part = leaves // LOADS
    bf16 = up_all.dtype

    loads = [pltpu.make_async_copy(transfer_hbm, transfer, load_sem.at[2, 0])]
    for c in range(LOADS):
        rows = pl.ds(c * part, part)
        loads.append(pltpu.make_async_copy(basis_hbm.at[rows], basis_in.at[rows], load_sem.at[0, c]))
        loads.append(pltpu.make_async_copy(charges_hbm.at[rows], charges.at[rows], load_sem.at[1, c]))
    for load in loads[1:] + loads[:1]:
        load.start()

    barrier = pltpu.get_barrier_semaphore()

    def greet(k, carry):
        pl.semaphore_signal(barrier, inc=1, device_id=(lax.rem(me + k, n),), device_id_type=MESH)
        return carry

    lax.fori_loop(1, n, greet, 0)
    near[leaves + side] = jnp.zeros((rank, rhs), bf16)
    parent_pool[parents + n] = jnp.zeros((rank, rhs), bf16)
    zeros[...] = jnp.zeros_like(zeros)
    for j in range(leaf_coupling.shape[0]):
        stacked[:, j * rank : (j + 1) * rank] = leaf_coupling[j]
    for j in range(parent_coupling.shape[0]):
        pstacked[:, j * rank : (j + 1) * rank] = parent_coupling[j]
    for load in loads[1:]:
        load.wait()
    pl.semaphore_wait(barrier, n - 1)

    def up(leaf):
        return jnp.dot(basis_in[leaf], charges[leaf], preferred_element_type=jnp.float32).astype(bf16)

    def far_copy(c):
        rows = pl.ds(c * piece, piece)
        return pltpu.make_async_remote_copy(
            src_ref=far_stage.at[rows],
            dst_ref=far_out.at[rows],
            send_sem=far_sem.at[0, c],
            recv_sem=far_sem.at[1, c],
            device_id=(far_target,),
            device_id_type=MESH,
        )

    def zero_copy(c):
        return pltpu.make_async_copy(zeros, far_out.at[pl.ds(c * piece, piece)], zero_sem.at[c])

    for c in range(CHUNKS):

        def fill_far(i, carry):
            far_stage[c * piece + i] = up(leaf_sends[me, odd, c * piece + i])
            return carry

        lax.fori_loop(0, piece, fill_far, 0, unroll=8)

        @pl.when(has_far)
        def _():
            far_copy(c).start()

        @pl.when(jnp.logical_not(has_far))
        def _():
            zero_copy(c).start()

    def up_row(leaf, carry):
        row = up(leaf)
        up_all[leaf] = row
        near[leaf] = row
        return carry

    lax.fori_loop(0, leaves, up_row, 0, unroll=8)
    loads[0].wait()

    def up_parent(p, carry):
        row = lax.dot_general(
            transfer[p].reshape(8 * rank, rank),
            up_all[pl.ds(8 * p, 8)].reshape(8 * rank, rhs),
            CONTRACT_FIRST,
            preferred_element_type=jnp.float32,
        ).astype(bf16)
        parent_all[p] = row
        parent_pool[p] = row
        return carry

    lax.fori_loop(0, parents, up_parent, 0, unroll=2)

    def fill_parent(d, carry):
        parent_stage[d] = parent_all[parent_sends[me, d]]
        return carry

    lax.fori_loop(0, n, fill_parent, 0)

    def parent_copy(k):
        target = lax.rem(me + k, n)
        return pltpu.make_async_remote_copy(
            src_ref=parent_stage.at[target],
            dst_ref=parent_pool.at[parents + me],
            send_sem=parent_send_sem.at[k],
            recv_sem=parent_recv_sem.at[k],
            device_id=(target,),
            device_id_type=MESH,
        )

    def start_parent(k, carry):
        parent_copy(k).start()
        return carry

    lax.fori_loop(1, n, start_parent, 0)
    parent_pool[parents + me] = parent_stage[me]

    def fill_fast(i, carry):
        fast_stage[i] = up_all[leaf_sends[me, 1 - odd, i]]
        return carry

    lax.fori_loop(0, side, fill_fast, 0, unroll=4)
    fast_copy = pltpu.make_async_remote_copy(
        src_ref=fast_stage,
        dst_ref=near.at[pl.ds(leaves, side)],
        send_sem=fast_sem.at[0],
        recv_sem=fast_sem.at[1],
        device_id=(fast_target,),
        device_id_type=MESH,
    )
    fast_copy.start()

    width = far_codes.shape[0]
    codes = [far_codes[j : j + 1, :] for j in range(width)]
    used = [code >= 0 for code in codes]
    place = jnp.zeros_like(codes[0])
    places = []
    for j in range(width):
        places.append(place)
        place = place + used[j].astype(jnp.int32)
    for p in range(width):
        entry = jnp.full_like(place, side)
        for j in range(p, width):
            entry = jnp.where(jnp.logical_and(used[j], places[j] == p), codes[j], entry)
        list_out[p : p + 1, :] = entry
    list_out[width : width + 1, :] = place

    fast_copy.wait()

    def near_pair(i, carry):
        pair = field_pair(2 * i, 2 * i + 1, near, near_slots, stacked)
        field[2 * i] = pair[:, :rhs]
        field[2 * i + 1] = pair[:, rhs:]
        return carry

    lax.fori_loop(0, leaves // 2, near_pair, 0, unroll=2)

    def wait_parent(k, carry):
        source = lax.rem(me - k + n, n)
        copy = pltpu.make_async_remote_copy(
            src_ref=parent_stage.at[lax.rem(me + k, n)],
            dst_ref=parent_pool.at[parents + source],
            send_sem=parent_send_sem.at[k],
            recv_sem=parent_recv_sem.at[k],
            device_id=(lax.rem(me + k, n),),
            device_id_type=MESH,
        )
        copy.wait_send()
        copy.wait_recv()
        return carry

    lax.fori_loop(1, n, wait_parent, 0)

    def parent_pair(i, carry):
        pair = field_pair(2 * i, 2 * i + 1, parent_pool, parent_slots, pstacked)
        down[2 * i] = pair[:, :rhs].astype(bf16)
        down[2 * i + 1] = pair[:, rhs:].astype(bf16)
        return carry

    lax.fori_loop(0, parents // 2, parent_pair, 0)

    def field_copy(c):
        rows = pl.ds(c * part, part)
        return pltpu.make_async_copy(field.at[rows], field_out.at[rows], field_sem.at[c])

    for c in range(LOADS):

        def push(i, carry):
            p = c * (parents // LOADS) + i
            pushed = jnp.dot(transfer[p].reshape(8 * rank, rank), down[p], preferred_element_type=jnp.float32)
            rows = pl.ds(8 * p, 8)
            field[rows] = field[rows] + pushed.reshape(8, rank, rhs)
            return carry

        lax.fori_loop(0, parents // LOADS, push, 0, unroll=2)
        field_copy(c).start()
    for c in range(LOADS):
        field_copy(c).wait()
    for c in range(CHUNKS):

        @pl.when(has_far)
        def _():
            far_copy(c).wait()

        @pl.when(jnp.logical_not(has_far))
        def _():
            zero_copy(c).wait()


def downward_kernel(lists, leaf_coupling, far, field, basis_out, potential, pool, even_side, odd_side, total, sem):
    step = pl.program_id(0)
    block, rank, rhs = total.shape
    side = far.shape[0]
    width = leaf_coupling.shape[0]

    @pl.when(step == 0)
    def _():
        copy = pltpu.make_async_copy(far, pool.at[pl.ds(0, side)], sem)
        copy.start()
        pool[side] = jnp.zeros((rank, rhs), pool.dtype)
        blank = jnp.zeros((rank, rank), pool.dtype)
        for j in range(width):
            even_side[j] = jnp.concatenate([leaf_coupling[j], blank], 1)
            odd_side[j] = jnp.concatenate([blank, leaf_coupling[j]], 1)
        copy.wait()

    def group(target, g):
        codes = [lists[GROUP * g + k, target] for k in range(GROUP)]
        slot = [lax.shift_right_logical(code, 10) for code in codes]
        left = [even_side[slot[k]] + odd_side[slot[k + 1]] for k in range(0, GROUP, 2)]
        rows = [pool[jnp.bitwise_and(code, CODE - 1)] for code in codes]
        return jnp.dot(jnp.concatenate(left, 1), jnp.concatenate(rows, 0), preferred_element_type=jnp.float32)

    for leaf in range(block):
        total[leaf] = field[leaf] + group(step * block + leaf, 0)

    def rest(leaf, carry):
        target = step * block + leaf
        groups = lax.shift_right_logical(lists[width, target] + (GROUP - 1), 2)

        def more(g, inner):
            total[leaf] += group(target, g)
            return inner

        lax.fori_loop(1, groups, more, 0)
        return carry

    lax.fori_loop(0, block, rest, 0)
    for leaf in range(block):
        potential[leaf] = lax.dot_general(
            basis_out[leaf], total[leaf].astype(jnp.bfloat16), CONTRACT_FIRST, preferred_element_type=jnp.float32
        ).astype(potential.dtype)


def shards(
    n,
    charges,
    basis_in,
    basis_out,
    transfer,
    leaf_coupling,
    parent_coupling,
    leaf_sources,
    leaf_counts,
    leaf_sends,
    parent_sources,
    parent_counts,
    parent_sends,
):
    leaves, points, rhs = charges.shape
    rank = basis_in.shape[1]
    parents = transfer.shape[0]
    side = leaf_sends.shape[2]
    width = leaf_sources.shape[1]
    pwidth = parent_sources.shape[1]
    block = 16
    bf16 = jnp.bfloat16
    odd = lax.rem(lax.axis_index("leaf"), 2)
    sources = leaf_sources.T
    slot = lax.broadcasted_iota(jnp.int32, sources.shape, 0)
    valid = slot < leaf_counts[None, :]
    fast_row = sources - (leaves + (1 - odd) * side)
    far_row = sources - (leaves + odd * side)
    in_fast = (fast_row >= 0) & (fast_row < side)
    in_far = (far_row >= 0) & (far_row < side)
    near_row = jnp.where(sources < leaves, sources, jnp.where(in_fast, leaves + fast_row, leaves + side))
    near_slots = jnp.where(valid, near_row, leaves + side)
    far_codes = jnp.where(valid & in_far & (sources >= leaves), slot * CODE + far_row, -1)
    psources = parent_sources.T
    pslot = lax.broadcasted_iota(jnp.int32, psources.shape, 0)
    parent_slots = jnp.where(pslot < parent_counts[None, :], psources, parents + n)
    list_rows = width + 8
    far, field, lists = pl.pallas_call(
        functools.partial(upward_kernel, n),
        out_shape=(
            jax.ShapeDtypeStruct((side, rank, rhs), bf16),
            jax.ShapeDtypeStruct((leaves, rank, rhs), jnp.float32),
            jax.ShapeDtypeStruct((list_rows, leaves), jnp.int32),
        ),
        in_specs=[ANY, ANY, ANY, SMEM, SMEM, SMEM, SMEM, VMEM, VMEM, VMEM],
        out_specs=(ANY, ANY, VMEM),
        scratch_shapes=[
            pltpu.VMEM((leaves, points, rhs), bf16),
            pltpu.VMEM((leaves, rank, points), bf16),
            pltpu.VMEM((parents, 8, rank, rank), bf16),
            pltpu.VMEM((leaves, rank, rhs), bf16),
            pltpu.VMEM((leaves + side + 1, rank, rhs), bf16),
            pltpu.VMEM((side, rank, rhs), bf16),
            pltpu.VMEM((side, rank, rhs), bf16),
            pltpu.VMEM((parents, rank, rhs), bf16),
            pltpu.VMEM((n, rank, rhs), bf16),
            pltpu.VMEM((parents + n + 1, rank, rhs), bf16),
            pltpu.VMEM((parents, rank, rhs), bf16),
            pltpu.VMEM((leaves, rank, rhs), jnp.float32),
            pltpu.VMEM((rank, width * rank), bf16),
            pltpu.VMEM((rank, pwidth * rank), bf16),
            pltpu.VMEM((side // CHUNKS, rank, rhs), bf16),
            pltpu.SemaphoreType.DMA((3, LOADS)),
            pltpu.SemaphoreType.DMA((2, CHUNKS)),
            pltpu.SemaphoreType.DMA((2,)),
            pltpu.SemaphoreType.DMA((n,)),
            pltpu.SemaphoreType.DMA((n,)),
            pltpu.SemaphoreType.DMA((CHUNKS,)),
            pltpu.SemaphoreType.DMA((LOADS,)),
        ],
        compiler_params=pltpu.CompilerParams(
            collective_id=0, has_side_effects=True, vmem_limit_bytes=56 * 2**20
        ),
        name="upward",
    )(
        charges,
        basis_in,
        transfer,
        leaf_sends,
        parent_sends,
        near_slots,
        parent_slots,
        far_codes,
        leaf_coupling,
        parent_coupling,
    )
    return pl.pallas_call(
        downward_kernel,
        out_shape=jax.ShapeDtypeStruct((leaves, points, rhs), bf16),
        grid_spec=pltpu.PrefetchScalarGridSpec(
            num_scalar_prefetch=1,
            grid=(leaves // block,),
            in_specs=[
                pl.BlockSpec(leaf_coupling.shape, lambda i, *_: (0, 0, 0)),
                ANY,
                pl.BlockSpec((block, rank, rhs), lambda i, *_: (i, 0, 0)),
                pl.BlockSpec((block, rank, points), lambda i, *_: (i, 0, 0)),
            ],
            out_specs=pl.BlockSpec((block, points, rhs), lambda i, *_: (i, 0, 0)),
            scratch_shapes=[
                pltpu.VMEM((side + 1, rank, rhs), bf16),
                pltpu.VMEM((width, rank, 2 * rank), bf16),
                pltpu.VMEM((width, rank, 2 * rank), bf16),
                pltpu.VMEM((block, rank, rhs), jnp.float32),
                pltpu.SemaphoreType.DMA,
            ],
        ),
        compiler_params=pltpu.CompilerParams(vmem_limit_bytes=60 * 2**20),
        name="downward",
    )(lists, leaf_coupling, far, field, basis_out)


def solution(mesh):
    return jax.shard_map(
        functools.partial(shards, mesh.shape["leaf"]),
        mesh=mesh,
        in_specs=(
            P("leaf", None, None),
            P("leaf", None, None),
            P("leaf", None, None),
            P("leaf", None, None, None),
            P(),
            P(),
            P("leaf", None),
            P("leaf"),
            P(),
            P("leaf", None),
            P("leaf"),
            P(),
        ),
        out_specs=P("leaf", None, None),
        check_vma=False,
    )
```

```python
import functools

import jax
import jax.numpy as jnp
from jax import lax
from jax.experimental import pallas as pl
from jax.experimental.pallas import tpu as pltpu
from jax.sharding import PartitionSpec as P

CHUNKS = 4
EARLY = 2
LOADS = 8
GROUP = 4
CODE = 1024
ANY = pl.BlockSpec(memory_space=pl.ANY)
SMEM = pl.BlockSpec(memory_space=pltpu.SMEM)
VMEM = pl.BlockSpec(memory_space=pltpu.VMEM)
CONTRACT_FIRST = (((0,), (0,)), ((), ()))
MESH = pl.DeviceIdType.MESH


def field_pair(first, second, pool, slots, stacked):
    columns = [
        jnp.concatenate([pool[slots[j, target]] for j in range(slots.shape[0])], 0) for target in (first, second)
    ]
    return jnp.dot(stacked[...], jnp.concatenate(columns, 1), preferred_element_type=jnp.float32)


def upward_kernel(
    n,
    charges_hbm,
    basis_hbm,
    transfer_hbm,
    leaf_sends,
    parent_sends,
    leaf_sources,
    leaf_counts,
    parent_sources,
    parent_counts,
    leaf_coupling,
    parent_coupling,
    far_out,
    field_out,
    list_out,
    charges,
    basis_in,
    transfer,
    up_all,
    near,
    far_stage,
    fast_stage,
    parent_all,
    parent_stage,
    parent_pool,
    down,
    field,
    stacked,
    pstacked,
    zeros,
    near_vector,
    parent_vector,
    near_slots,
    parent_slots,
    load_sem,
    far_sem,
    fast_sem,
    parent_send_sem,
    parent_recv_sem,
    zero_sem,
    field_sem,
    slot_sem,
):
    me = lax.axis_index("leaf")
    odd = lax.rem(me, 2)
    fast_target = me + 1 - 2 * odd
    far_target = me - 1 + 2 * odd
    has_far = jnp.logical_and(far_target >= 0, far_target < n)
    leaves, rank, rhs = up_all.shape
    parents = parent_all.shape[0]
    side = far_stage.shape[0]
    piece = side // CHUNKS
    part = leaves // LOADS
    bf16 = up_all.dtype

    loads = [pltpu.make_async_copy(transfer_hbm, transfer, load_sem.at[2, 0])]
    for c in range(LOADS):
        rows = pl.ds(c * part, part)
        loads.append(pltpu.make_async_copy(basis_hbm.at[rows], basis_in.at[rows], load_sem.at[0, c]))
        loads.append(pltpu.make_async_copy(charges_hbm.at[rows], charges.at[rows], load_sem.at[1, c]))
    for load in loads[1:] + loads[:1]:
        load.start()

    barrier = pltpu.get_barrier_semaphore()

    def greet(k, carry):
        pl.semaphore_signal(barrier, inc=1, device_id=(lax.rem(me + k, n),), device_id_type=MESH)
        return carry

    lax.fori_loop(1, n, greet, 0)
    near[leaves + side] = jnp.zeros((rank, rhs), bf16)
    parent_pool[parents + n] = jnp.zeros((rank, rhs), bf16)
    zeros[...] = jnp.zeros_like(zeros)
    for j in range(leaf_coupling.shape[0]):
        stacked[:, j * rank : (j + 1) * rank] = leaf_coupling[j]
    for j in range(parent_coupling.shape[0]):
        pstacked[:, j * rank : (j + 1) * rank] = parent_coupling[j]
    width = leaf_sources.shape[0]
    limit = leaf_counts[...]
    codes, used = [], []
    for j in range(width):
        source = leaf_sources[j : j + 1, :]
        valid = limit > j
        fast_row = source - (leaves + (1 - odd) * side)
        far_row = source - (leaves + odd * side)
        row = jnp.where(
            source < leaves,
            source,
            jnp.where(jnp.logical_and(fast_row >= 0, fast_row < side), leaves + fast_row, leaves + side),
        )
        near_vector[j : j + 1, :] = jnp.where(valid, row, leaves + side)
        codes.append(j * CODE + far_row)
        used.append(jnp.logical_and(valid, jnp.logical_and(far_row >= 0, far_row < side)))
    parent_vector[...] = jnp.zeros_like(parent_vector)
    parent_limit = parent_counts[...]
    for j in range(parent_sources.shape[0]):
        parent_vector[j : j + 1, 0:parents] = jnp.where(parent_limit > j, parent_sources[j : j + 1, :], parents + n)
    slot_copies = [
        pltpu.make_async_copy(near_vector, near_slots, slot_sem.at[0]),
        pltpu.make_async_copy(parent_vector, parent_slots, slot_sem.at[1]),
    ]
    for copy in slot_copies:
        copy.start()

    place = jnp.zeros_like(limit)
    places = []
    for j in range(width):
        places.append(place)
        place = place + used[j].astype(jnp.int32)
    for p in range(width):
        entry = jnp.full_like(place, side)
        for j in range(p, width):
            entry = jnp.where(jnp.logical_and(used[j], places[j] == p), codes[j], entry)
        list_out[p : p + 1, :] = entry
    list_out[width : width + 1, :] = place
    for copy in slot_copies:
        copy.wait()
    for load in loads[1:]:
        load.wait()
    pl.semaphore_wait(barrier, n - 1)

    def up(leaf):
        return jnp.dot(basis_in[leaf], charges[leaf], preferred_element_type=jnp.float32).astype(bf16)

    def far_copy(c):
        rows = pl.ds(c * piece, piece)
        return pltpu.make_async_remote_copy(
            src_ref=far_stage.at[rows],
            dst_ref=far_out.at[rows],
            send_sem=far_sem.at[0, c],
            recv_sem=far_sem.at[1, c],
            device_id=(far_target,),
            device_id_type=MESH,
        )

    def zero_copy(c):
        return pltpu.make_async_copy(zeros, far_out.at[pl.ds(c * piece, piece)], zero_sem.at[c])

    def send_far(c, value):
        def fill_far(i, carry):
            far_stage[c * piece + i] = value(leaf_sends[me, odd, c * piece + i])
            return carry

        lax.fori_loop(0, piece, fill_far, 0, unroll=8)

        @pl.when(has_far)
        def _():
            far_copy(c).start()

        @pl.when(jnp.logical_not(has_far))
        def _():
            zero_copy(c).start()

    for c in range(EARLY):
        send_far(c, up)

    def up_row(leaf, carry):
        row = up(leaf)
        up_all[leaf] = row
        near[leaf] = row
        return carry

    lax.fori_loop(0, leaves, up_row, 0, unroll=8)
    def fill_fast(i, carry):
        fast_stage[i] = up_all[leaf_sends[me, 1 - odd, i]]
        return carry

    lax.fori_loop(0, side, fill_fast, 0, unroll=4)
    fast_copy = pltpu.make_async_remote_copy(
        src_ref=fast_stage,
        dst_ref=near.at[pl.ds(leaves, side)],
        send_sem=fast_sem.at[0],
        recv_sem=fast_sem.at[1],
        device_id=(fast_target,),
        device_id_type=MESH,
    )
    fast_copy.start()

    loads[0].wait()

    def up_parent(p, carry):
        row = lax.dot_general(
            transfer[p].reshape(8 * rank, rank),
            up_all[pl.ds(8 * p, 8)].reshape(8 * rank, rhs),
            CONTRACT_FIRST,
            preferred_element_type=jnp.float32,
        ).astype(bf16)
        parent_all[p] = row
        parent_pool[p] = row
        return carry

    lax.fori_loop(0, parents, up_parent, 0, unroll=2)

    def fill_parent(d, carry):
        parent_stage[d] = parent_all[parent_sends[me, d]]
        return carry

    lax.fori_loop(0, n, fill_parent, 0)

    def parent_copy(k):
        target = lax.rem(me + k, n)
        return pltpu.make_async_remote_copy(
            src_ref=parent_stage.at[target],
            dst_ref=parent_pool.at[parents + me],
            send_sem=parent_send_sem.at[k],
            recv_sem=parent_recv_sem.at[k],
            device_id=(target,),
            device_id_type=MESH,
        )

    def start_parent(k, carry):
        parent_copy(k).start()
        return carry

    lax.fori_loop(1, n, start_parent, 0)
    parent_pool[parents + me] = parent_stage[me]

    for c in range(EARLY, CHUNKS):
        send_far(c, lambda leaf: up_all[leaf])
    fast_copy.wait()

    def near_pair(i, carry):
        pair = field_pair(2 * i, 2 * i + 1, near, near_slots, stacked)
        field[2 * i] = pair[:, :rhs]
        field[2 * i + 1] = pair[:, rhs:]
        return carry

    lax.fori_loop(0, leaves // 2, near_pair, 0, unroll=2)

    def wait_parent(k, carry):
        source = lax.rem(me - k + n, n)
        copy = pltpu.make_async_remote_copy(
            src_ref=parent_stage.at[lax.rem(me + k, n)],
            dst_ref=parent_pool.at[parents + source],
            send_sem=parent_send_sem.at[k],
            recv_sem=parent_recv_sem.at[k],
            device_id=(lax.rem(me + k, n),),
            device_id_type=MESH,
        )
        copy.wait_send()
        copy.wait_recv()
        return carry

    lax.fori_loop(1, n, wait_parent, 0)

    def parent_pair(i, carry):
        pair = field_pair(2 * i, 2 * i + 1, parent_pool, parent_slots, pstacked)
        down[2 * i] = pair[:, :rhs].astype(bf16)
        down[2 * i + 1] = pair[:, rhs:].astype(bf16)
        return carry

    lax.fori_loop(0, parents // 2, parent_pair, 0)

    def field_copy(c):
        rows = pl.ds(c * part, part)
        return pltpu.make_async_copy(field.at[rows], field_out.at[rows], field_sem.at[c])

    for c in range(LOADS):

        def push(i, carry):
            p = c * (parents // LOADS) + i
            pushed = jnp.dot(transfer[p].reshape(8 * rank, rank), down[p], preferred_element_type=jnp.float32)
            rows = pl.ds(8 * p, 8)
            field[rows] = field[rows] + pushed.reshape(8, rank, rhs)
            return carry

        lax.fori_loop(0, parents // LOADS, push, 0, unroll=2)
        field_copy(c).start()
    for c in range(LOADS):
        field_copy(c).wait()
    for c in range(CHUNKS):

        @pl.when(has_far)
        def _():
            far_copy(c).wait()

        @pl.when(jnp.logical_not(has_far))
        def _():
            zero_copy(c).wait()


def downward_kernel(lists, leaf_coupling, far, field, basis_out, potential, pool, even_side, odd_side, total, sem):
    step = pl.program_id(0)
    block, rank, rhs = total.shape
    side = far.shape[0]
    width = leaf_coupling.shape[0]

    @pl.when(step == 0)
    def _():
        copy = pltpu.make_async_copy(far, pool.at[pl.ds(0, side)], sem)
        copy.start()
        pool[side] = jnp.zeros((rank, rhs), pool.dtype)
        blank = jnp.zeros((rank, rank), pool.dtype)
        for j in range(width):
            even_side[j] = jnp.concatenate([leaf_coupling[j], blank], 1)
            odd_side[j] = jnp.concatenate([blank, leaf_coupling[j]], 1)
        copy.wait()

    def group(target, g):
        codes = [lists[GROUP * g + k, target] for k in range(GROUP)]
        slot = [lax.shift_right_logical(code, 10) for code in codes]
        left = [even_side[slot[k]] + odd_side[slot[k + 1]] for k in range(0, GROUP, 2)]
        rows = [pool[jnp.bitwise_and(code, CODE - 1)] for code in codes]
        return jnp.dot(jnp.concatenate(left, 1), jnp.concatenate(rows, 0), preferred_element_type=jnp.float32)

    for leaf in range(block):
        total[leaf] = field[leaf] + group(step * block + leaf, 0)

    def rest(leaf):
        target = step * block + leaf
        count = lists[width, target]

        @pl.when(count > GROUP)
        def _():
            def more(g, carry):
                total[leaf] += group(target, g)
                return carry

            lax.fori_loop(1, lax.shift_right_logical(count + (GROUP - 1), 2), more, 0)

    for leaf in range(block):
        rest(leaf)
    for leaf in range(block):
        potential[leaf] = lax.dot_general(
            basis_out[leaf], total[leaf].astype(jnp.bfloat16), CONTRACT_FIRST, preferred_element_type=jnp.float32
        ).astype(potential.dtype)


def shards(
    n,
    charges,
    basis_in,
    basis_out,
    transfer,
    leaf_coupling,
    parent_coupling,
    leaf_sources,
    leaf_counts,
    leaf_sends,
    parent_sources,
    parent_counts,
    parent_sends,
):
    leaves, points, rhs = charges.shape
    rank = basis_in.shape[1]
    parents = transfer.shape[0]
    side = leaf_sends.shape[2]
    width = leaf_sources.shape[1]
    pwidth = parent_sources.shape[1]
    block = 32
    bf16 = jnp.bfloat16
    list_rows = width + 8
    far, field, lists = pl.pallas_call(
        functools.partial(upward_kernel, n),
        out_shape=(
            jax.ShapeDtypeStruct((side, rank, rhs), bf16),
            jax.ShapeDtypeStruct((leaves, rank, rhs), jnp.float32),
            jax.ShapeDtypeStruct((list_rows, leaves), jnp.int32),
        ),
        in_specs=[ANY, ANY, ANY, SMEM, SMEM] + [VMEM] * 6,
        out_specs=(ANY, ANY, VMEM),
        scratch_shapes=[
            pltpu.VMEM((leaves, points, rhs), bf16),
            pltpu.VMEM((leaves, rank, points), bf16),
            pltpu.VMEM((parents, 8, rank, rank), bf16),
            pltpu.VMEM((leaves, rank, rhs), bf16),
            pltpu.VMEM((leaves + side + 1, rank, rhs), bf16),
            pltpu.VMEM((side, rank, rhs), bf16),
            pltpu.VMEM((side, rank, rhs), bf16),
            pltpu.VMEM((parents, rank, rhs), bf16),
            pltpu.VMEM((n, rank, rhs), bf16),
            pltpu.VMEM((parents + n + 1, rank, rhs), bf16),
            pltpu.VMEM((parents, rank, rhs), bf16),
            pltpu.VMEM((leaves, rank, rhs), jnp.float32),
            pltpu.VMEM((rank, width * rank), bf16),
            pltpu.VMEM((rank, pwidth * rank), bf16),
            pltpu.VMEM((side // CHUNKS, rank, rhs), bf16),
            pltpu.VMEM((width, leaves), jnp.int32),
            pltpu.VMEM((pwidth, -(-parents // 128) * 128), jnp.int32),
            pltpu.SMEM((width, leaves), jnp.int32),
            pltpu.SMEM((pwidth, -(-parents // 128) * 128), jnp.int32),
            pltpu.SemaphoreType.DMA((3, LOADS)),
            pltpu.SemaphoreType.DMA((2, CHUNKS)),
            pltpu.SemaphoreType.DMA((2,)),
            pltpu.SemaphoreType.DMA((n,)),
            pltpu.SemaphoreType.DMA((n,)),
            pltpu.SemaphoreType.DMA((CHUNKS,)),
            pltpu.SemaphoreType.DMA((LOADS,)),
            pltpu.SemaphoreType.DMA((2,)),
        ],
        compiler_params=pltpu.CompilerParams(
            collective_id=0, has_side_effects=True, vmem_limit_bytes=56 * 2**20
        ),
        name="upward",
    )(
        charges,
        basis_in,
        transfer,
        leaf_sends,
        parent_sends,
        leaf_sources.T,
        leaf_counts[None, :],
        parent_sources.T,
        parent_counts[None, :],
        leaf_coupling,
        parent_coupling,
    )
    return pl.pallas_call(
        downward_kernel,
        out_shape=jax.ShapeDtypeStruct((leaves, points, rhs), bf16),
        grid_spec=pltpu.PrefetchScalarGridSpec(
            num_scalar_prefetch=1,
            grid=(leaves // block,),
            in_specs=[
                pl.BlockSpec(leaf_coupling.shape, lambda i, *_: (0, 0, 0)),
                ANY,
                pl.BlockSpec((block, rank, rhs), lambda i, *_: (i, 0, 0)),
                pl.BlockSpec((block, rank, points), lambda i, *_: (i, 0, 0)),
            ],
            out_specs=pl.BlockSpec((block, points, rhs), lambda i, *_: (i, 0, 0)),
            scratch_shapes=[
                pltpu.VMEM((side + 1, rank, rhs), bf16),
                pltpu.VMEM((width, rank, 2 * rank), bf16),
                pltpu.VMEM((width, rank, 2 * rank), bf16),
                pltpu.VMEM((block, rank, rhs), jnp.float32),
                pltpu.SemaphoreType.DMA,
            ],
        ),
        compiler_params=pltpu.CompilerParams(vmem_limit_bytes=60 * 2**20),
        name="downward",
    )(lists, leaf_coupling, far, field, basis_out)


def solution(mesh):
    return jax.shard_map(
        functools.partial(shards, mesh.shape["leaf"]),
        mesh=mesh,
        in_specs=(
            P("leaf", None, None),
            P("leaf", None, None),
            P("leaf", None, None),
            P("leaf", None, None, None),
            P(),
            P(),
            P("leaf", None),
            P("leaf"),
            P(),
            P("leaf", None),
            P("leaf"),
            P(),
        ),
        out_specs=P("leaf", None, None),
        check_vma=False,
    )
```

```python
import functools

import jax
import jax.numpy as jnp
from jax import lax
from jax.experimental import pallas as pl
from jax.experimental.pallas import tpu as pltpu
from jax.sharding import PartitionSpec as P

CHUNKS = 4
EARLY = 2
LOADS = 8
GROUP = 4
CODE = 1024
ANY = pl.BlockSpec(memory_space=pl.ANY)
SMEM = pl.BlockSpec(memory_space=pltpu.SMEM)
VMEM = pl.BlockSpec(memory_space=pltpu.VMEM)
CONTRACT_FIRST = (((0,), (0,)), ((), ()))
MESH = pl.DeviceIdType.MESH


def field_pair(first, second, pool, slots, stacked):
    columns = [
        jnp.concatenate([pool[slots[j, target]] for j in range(slots.shape[0])], 0) for target in (first, second)
    ]
    return jnp.dot(stacked[...], jnp.concatenate(columns, 1), preferred_element_type=jnp.float32)


def upward_kernel(
    n,
    charges_hbm,
    basis_hbm,
    transfer_hbm,
    leaf_sends,
    parent_sends,
    leaf_sources,
    leaf_counts,
    parent_sources,
    parent_counts,
    leaf_coupling,
    parent_coupling,
    far_out,
    field_out,
    list_out,
    charges,
    basis_in,
    transfer,
    up_all,
    near,
    far_stage,
    fast_stage,
    parent_all,
    parent_stage,
    parent_pool,
    down,
    field,
    stacked,
    pstacked,
    zeros,
    near_vector,
    parent_vector,
    near_slots,
    parent_slots,
    load_sem,
    far_sem,
    fast_sem,
    parent_send_sem,
    parent_recv_sem,
    zero_sem,
    field_sem,
    slot_sem,
):
    me = lax.axis_index("leaf")
    odd = lax.rem(me, 2)
    fast_target = me + 1 - 2 * odd
    far_target = me - 1 + 2 * odd
    has_far = jnp.logical_and(far_target >= 0, far_target < n)
    leaves, rank, rhs = up_all.shape
    parents = parent_all.shape[0]
    side = far_stage.shape[0]
    piece = side // CHUNKS
    part = leaves // LOADS
    bf16 = up_all.dtype

    loads = [pltpu.make_async_copy(transfer_hbm, transfer, load_sem.at[2, 0])]
    for c in range(LOADS):
        rows = pl.ds(c * part, part)
        loads.append(pltpu.make_async_copy(basis_hbm.at[rows], basis_in.at[rows], load_sem.at[0, c]))
        loads.append(pltpu.make_async_copy(charges_hbm.at[rows], charges.at[rows], load_sem.at[1, c]))
    for load in loads[1:] + loads[:1]:
        load.start()

    barrier = pltpu.get_barrier_semaphore()

    def greet(k, carry):
        pl.semaphore_signal(barrier, inc=1, device_id=(lax.rem(me + k, n),), device_id_type=MESH)
        return carry

    lax.fori_loop(1, n, greet, 0)
    early = EARLY * piece
    spare = leaves + side + early
    near[spare] = jnp.zeros((rank, rhs), bf16)
    parent_pool[parents + n] = jnp.zeros((rank, rhs), bf16)
    zeros[...] = jnp.zeros_like(zeros)
    for j in range(leaf_coupling.shape[0]):
        stacked[:, j * rank : (j + 1) * rank] = leaf_coupling[j]
    for j in range(parent_coupling.shape[0]):
        pstacked[:, j * rank : (j + 1) * rank] = parent_coupling[j]
    width = leaf_sources.shape[0]
    limit = leaf_counts[...]
    codes, used = [], []
    for j in range(width):
        source = leaf_sources[j : j + 1, :]
        valid = limit > j
        fast_row = source - (leaves + (1 - odd) * side)
        far_row = source - (leaves + odd * side)
        row = jnp.where(
            source < leaves,
            source,
            jnp.where(
                jnp.logical_and(fast_row >= 0, fast_row < side),
                leaves + fast_row,
                jnp.where(jnp.logical_and(far_row >= 0, far_row < early), leaves + side + far_row, spare),
            ),
        )
        near_vector[j : j + 1, :] = jnp.where(valid, row, spare)
        codes.append(j * CODE + far_row - early)
        used.append(jnp.logical_and(valid, jnp.logical_and(far_row >= early, far_row < side)))
    parent_vector[...] = jnp.zeros_like(parent_vector)
    parent_limit = parent_counts[...]
    for j in range(parent_sources.shape[0]):
        parent_vector[j : j + 1, 0:parents] = jnp.where(parent_limit > j, parent_sources[j : j + 1, :], parents + n)
    slot_copies = [
        pltpu.make_async_copy(near_vector, near_slots, slot_sem.at[0]),
        pltpu.make_async_copy(parent_vector, parent_slots, slot_sem.at[1]),
    ]
    for copy in slot_copies:
        copy.start()

    place = jnp.zeros_like(limit)
    places = []
    for j in range(width):
        places.append(place)
        place = place + used[j].astype(jnp.int32)
    for p in range(width):
        entry = jnp.full_like(place, side - early)
        for j in range(p, width):
            entry = jnp.where(jnp.logical_and(used[j], places[j] == p), codes[j], entry)
        list_out[p : p + 1, :] = entry
    list_out[width : width + 1, :] = place
    for copy in slot_copies:
        copy.wait()
    for load in loads[1:]:
        load.wait()
    pl.semaphore_wait(barrier, n - 1)

    def up(first, second):
        both = jnp.dot(
            jnp.concatenate([basis_in[first], basis_in[second]], 0),
            jnp.concatenate([charges[first], charges[second]], 1),
            preferred_element_type=jnp.float32,
        )
        return both[:rank, :rhs].astype(bf16), both[rank:, rhs:].astype(bf16)

    def landing(c):
        if c < EARLY:
            return near.at[pl.ds(leaves + side + c * piece, piece)]
        return far_out.at[pl.ds((c - EARLY) * piece, piece)]

    def far_copy(c):
        rows = pl.ds(c * piece, piece)
        return pltpu.make_async_remote_copy(
            src_ref=far_stage.at[rows],
            dst_ref=landing(c),
            send_sem=far_sem.at[0, c],
            recv_sem=far_sem.at[1, c],
            device_id=(far_target,),
            device_id_type=MESH,
        )

    def zero_copy(c):
        return pltpu.make_async_copy(zeros, landing(c), zero_sem.at[c])

    def send_far(c, value):
        def fill_far(i, carry):
            at = c * piece + 2 * i
            far_stage[at], far_stage[at + 1] = value(leaf_sends[me, odd, at], leaf_sends[me, odd, at + 1])
            return carry

        lax.fori_loop(0, piece // 2, fill_far, 0, unroll=4)

        @pl.when(has_far)
        def _():
            far_copy(c).start()

        @pl.when(jnp.logical_not(has_far))
        def _():
            zero_copy(c).start()

    for c in range(EARLY):
        send_far(c, up)

    def up_rows(i, carry):
        for leaf, row in zip((2 * i, 2 * i + 1), up(2 * i, 2 * i + 1)):
            up_all[leaf] = row
            near[leaf] = row
        return carry

    lax.fori_loop(0, leaves // 2, up_rows, 0, unroll=4)
    def fill_fast(i, carry):
        fast_stage[i] = up_all[leaf_sends[me, 1 - odd, i]]
        return carry

    lax.fori_loop(0, side, fill_fast, 0, unroll=4)
    fast_copy = pltpu.make_async_remote_copy(
        src_ref=fast_stage,
        dst_ref=near.at[pl.ds(leaves, side)],
        send_sem=fast_sem.at[0],
        recv_sem=fast_sem.at[1],
        device_id=(fast_target,),
        device_id_type=MESH,
    )
    fast_copy.start()

    loads[0].wait()

    def up_parent(p, carry):
        row = lax.dot_general(
            transfer[p].reshape(8 * rank, rank),
            up_all[pl.ds(8 * p, 8)].reshape(8 * rank, rhs),
            CONTRACT_FIRST,
            preferred_element_type=jnp.float32,
        ).astype(bf16)
        parent_all[p] = row
        parent_pool[p] = row
        return carry

    lax.fori_loop(0, parents, up_parent, 0, unroll=2)

    def fill_parent(d, carry):
        parent_stage[d] = parent_all[parent_sends[me, d]]
        return carry

    lax.fori_loop(0, n, fill_parent, 0)

    def parent_copy(k):
        target = lax.rem(me + k, n)
        return pltpu.make_async_remote_copy(
            src_ref=parent_stage.at[target],
            dst_ref=parent_pool.at[parents + me],
            send_sem=parent_send_sem.at[k],
            recv_sem=parent_recv_sem.at[k],
            device_id=(target,),
            device_id_type=MESH,
        )

    def start_parent(k, carry):
        parent_copy(k).start()
        return carry

    lax.fori_loop(1, n, start_parent, 0)
    parent_pool[parents + me] = parent_stage[me]

    for c in range(EARLY, CHUNKS):
        send_far(c, lambda first, second: (up_all[first], up_all[second]))
    fast_copy.wait()
    for c in range(EARLY):

        @pl.when(has_far)
        def _():
            far_copy(c).wait_recv()

        @pl.when(jnp.logical_not(has_far))
        def _():
            zero_copy(c).wait()


    def near_pair(i, carry):
        pair = field_pair(2 * i, 2 * i + 1, near, near_slots, stacked)
        field[2 * i] = pair[:, :rhs]
        field[2 * i + 1] = pair[:, rhs:]
        return carry

    lax.fori_loop(0, leaves // 2, near_pair, 0, unroll=2)

    def wait_parent(k, carry):
        source = lax.rem(me - k + n, n)
        copy = pltpu.make_async_remote_copy(
            src_ref=parent_stage.at[lax.rem(me + k, n)],
            dst_ref=parent_pool.at[parents + source],
            send_sem=parent_send_sem.at[k],
            recv_sem=parent_recv_sem.at[k],
            device_id=(lax.rem(me + k, n),),
            device_id_type=MESH,
        )
        copy.wait_send()
        copy.wait_recv()
        return carry

    lax.fori_loop(1, n, wait_parent, 0)

    def parent_pair(i, carry):
        pair = field_pair(2 * i, 2 * i + 1, parent_pool, parent_slots, pstacked)
        down[2 * i] = pair[:, :rhs].astype(bf16)
        down[2 * i + 1] = pair[:, rhs:].astype(bf16)
        return carry

    lax.fori_loop(0, parents // 2, parent_pair, 0)

    def field_copy(c):
        rows = pl.ds(c * part, part)
        return pltpu.make_async_copy(field.at[rows], field_out.at[rows], field_sem.at[c])

    for c in range(LOADS):

        def push(i, carry):
            p = c * (parents // LOADS) + i
            pushed = jnp.dot(transfer[p].reshape(8 * rank, rank), down[p], preferred_element_type=jnp.float32)
            rows = pl.ds(8 * p, 8)
            field[rows] = field[rows] + pushed.reshape(8, rank, rhs)
            return carry

        lax.fori_loop(0, parents // LOADS, push, 0, unroll=2)
        field_copy(c).start()
    for c in range(LOADS):
        field_copy(c).wait()
    for c in range(CHUNKS):

        @pl.when(has_far)
        def _():
            far_copy(c).wait_send()

    for c in range(EARLY, CHUNKS):

        @pl.when(has_far)
        def _():
            far_copy(c).wait_recv()

        @pl.when(jnp.logical_not(has_far))
        def _():
            zero_copy(c).wait()


def downward_kernel(lists, leaf_coupling, far, field, basis_out, potential, pool, even_side, odd_side, total, sem):
    step = pl.program_id(0)
    block, rank, rhs = total.shape
    side = far.shape[0]
    width = leaf_coupling.shape[0]

    @pl.when(step == 0)
    def _():
        copy = pltpu.make_async_copy(far, pool.at[pl.ds(0, side)], sem)
        copy.start()
        pool[side] = jnp.zeros((rank, rhs), pool.dtype)
        blank = jnp.zeros((rank, rank), pool.dtype)
        for j in range(width):
            even_side[j] = jnp.concatenate([leaf_coupling[j], blank], 1)
            odd_side[j] = jnp.concatenate([blank, leaf_coupling[j]], 1)
        copy.wait()

    def group(targets, g):
        left, right = [], []
        for target in targets:
            codes = [lists[GROUP * g + k, target] for k in range(GROUP)]
            slot = [lax.shift_right_logical(code, 10) for code in codes]
            sides = [even_side[slot[k]] + odd_side[slot[k + 1]] for k in range(0, GROUP, 2)]
            left.append(jnp.concatenate(sides, 1))
            right.append(jnp.concatenate([pool[jnp.bitwise_and(code, CODE - 1)] for code in codes], 0))
        product = jnp.dot(
            jnp.concatenate(left, 0), jnp.concatenate(right, 1), preferred_element_type=jnp.float32
        )
        return [product[k * rank : (k + 1) * rank, k * rhs : (k + 1) * rhs] for k in range(len(targets))]

    for leaf in range(0, block, 2):
        target = step * block + leaf
        first, second = group((target, target + 1), 0)
        total[leaf] = field[leaf] + first
        total[leaf + 1] = field[leaf + 1] + second

    def rest(leaf):
        target = step * block + leaf
        count = lists[width, target]

        @pl.when(count > GROUP)
        def _():
            def more(g, carry):
                total[leaf] += group((target,), g)[0]
                return carry

            lax.fori_loop(1, lax.shift_right_logical(count + (GROUP - 1), 2), more, 0)

    for leaf in range(block):
        rest(leaf)
    blank = jnp.zeros((rank, rhs), jnp.bfloat16)
    for leaf in range(0, block, 2):
        first, second = (total[leaf + k].astype(jnp.bfloat16) for k in range(2))
        diagonal = jnp.concatenate(
            [jnp.concatenate([first, blank], 1), jnp.concatenate([blank, second], 1)], 0
        )
        both = lax.dot_general(
            basis_out[leaf : leaf + 2].reshape(2 * rank, basis_out.shape[2]),
            diagonal,
            CONTRACT_FIRST,
            preferred_element_type=jnp.float32,
        ).astype(potential.dtype)
        potential[leaf] = both[:, :rhs]
        potential[leaf + 1] = both[:, rhs:]


def shards(
    n,
    charges,
    basis_in,
    basis_out,
    transfer,
    leaf_coupling,
    parent_coupling,
    leaf_sources,
    leaf_counts,
    leaf_sends,
    parent_sources,
    parent_counts,
    parent_sends,
):
    leaves, points, rhs = charges.shape
    rank = basis_in.shape[1]
    parents = transfer.shape[0]
    side = leaf_sends.shape[2]
    width = leaf_sources.shape[1]
    pwidth = parent_sources.shape[1]
    block = 32
    bf16 = jnp.bfloat16
    list_rows = width + 8
    early = EARLY * (side // CHUNKS)
    far, field, lists = pl.pallas_call(
        functools.partial(upward_kernel, n),
        out_shape=(
            jax.ShapeDtypeStruct((side - early, rank, rhs), bf16),
            jax.ShapeDtypeStruct((leaves, rank, rhs), jnp.float32),
            jax.ShapeDtypeStruct((list_rows, leaves), jnp.int32),
        ),
        in_specs=[ANY, ANY, ANY, SMEM, SMEM] + [VMEM] * 6,
        out_specs=(ANY, ANY, VMEM),
        scratch_shapes=[
            pltpu.VMEM((leaves, points, rhs), bf16),
            pltpu.VMEM((leaves, rank, points), bf16),
            pltpu.VMEM((parents, 8, rank, rank), bf16),
            pltpu.VMEM((leaves, rank, rhs), bf16),
            pltpu.VMEM((leaves + side + early + 1, rank, rhs), bf16),
            pltpu.VMEM((side, rank, rhs), bf16),
            pltpu.VMEM((side, rank, rhs), bf16),
            pltpu.VMEM((parents, rank, rhs), bf16),
            pltpu.VMEM((n, rank, rhs), bf16),
            pltpu.VMEM((parents + n + 1, rank, rhs), bf16),
            pltpu.VMEM((parents, rank, rhs), bf16),
            pltpu.VMEM((leaves, rank, rhs), jnp.float32),
            pltpu.VMEM((rank, width * rank), bf16),
            pltpu.VMEM((rank, pwidth * rank), bf16),
            pltpu.VMEM((side // CHUNKS, rank, rhs), bf16),
            pltpu.VMEM((width, leaves), jnp.int32),
            pltpu.VMEM((pwidth, -(-parents // 128) * 128), jnp.int32),
            pltpu.SMEM((width, leaves), jnp.int32),
            pltpu.SMEM((pwidth, -(-parents // 128) * 128), jnp.int32),
            pltpu.SemaphoreType.DMA((3, LOADS)),
            pltpu.SemaphoreType.DMA((2, CHUNKS)),
            pltpu.SemaphoreType.DMA((2,)),
            pltpu.SemaphoreType.DMA((n,)),
            pltpu.SemaphoreType.DMA((n,)),
            pltpu.SemaphoreType.DMA((CHUNKS,)),
            pltpu.SemaphoreType.DMA((LOADS,)),
            pltpu.SemaphoreType.DMA((2,)),
        ],
        compiler_params=pltpu.CompilerParams(
            collective_id=0, has_side_effects=True, vmem_limit_bytes=56 * 2**20
        ),
        name="upward",
    )(
        charges,
        basis_in,
        transfer,
        leaf_sends,
        parent_sends,
        leaf_sources.T,
        leaf_counts[None, :],
        parent_sources.T,
        parent_counts[None, :],
        leaf_coupling,
        parent_coupling,
    )
    return pl.pallas_call(
        downward_kernel,
        out_shape=jax.ShapeDtypeStruct((leaves, points, rhs), bf16),
        grid_spec=pltpu.PrefetchScalarGridSpec(
            num_scalar_prefetch=1,
            grid=(leaves // block,),
            in_specs=[
                pl.BlockSpec(leaf_coupling.shape, lambda i, *_: (0, 0, 0)),
                ANY,
                pl.BlockSpec((block, rank, rhs), lambda i, *_: (i, 0, 0)),
                pl.BlockSpec((block, rank, points), lambda i, *_: (i, 0, 0)),
            ],
            out_specs=pl.BlockSpec((block, points, rhs), lambda i, *_: (i, 0, 0)),
            scratch_shapes=[
                pltpu.VMEM((side - early + 1, rank, rhs), bf16),
                pltpu.VMEM((width, rank, 2 * rank), bf16),
                pltpu.VMEM((width, rank, 2 * rank), bf16),
                pltpu.VMEM((block, rank, rhs), jnp.float32),
                pltpu.SemaphoreType.DMA,
            ],
        ),
        compiler_params=pltpu.CompilerParams(vmem_limit_bytes=60 * 2**20),
        name="downward",
    )(lists, leaf_coupling, far, field, basis_out)


def solution(mesh):
    return jax.shard_map(
        functools.partial(shards, mesh.shape["leaf"]),
        mesh=mesh,
        in_specs=(
            P("leaf", None, None),
            P("leaf", None, None),
            P("leaf", None, None),
            P("leaf", None, None, None),
            P(),
            P(),
            P("leaf", None),
            P("leaf"),
            P(),
            P("leaf", None),
            P("leaf"),
            P(),
        ),
        out_specs=P("leaf", None, None),
        check_vma=False,
    )
```

```python
import functools

import jax
import jax.numpy as jnp
from jax import lax
from jax.experimental import pallas as pl
from jax.experimental.pallas import tpu as pltpu
from jax.sharding import PartitionSpec as P

CHUNKS = 4
EARLY = 1
LOADS = 8
GROUP = 4
CODE = 1024
ANY = pl.BlockSpec(memory_space=pl.ANY)
SMEM = pl.BlockSpec(memory_space=pltpu.SMEM)
VMEM = pl.BlockSpec(memory_space=pltpu.VMEM)
CONTRACT_FIRST = (((0,), (0,)), ((), ()))
MESH = pl.DeviceIdType.MESH


def field_pair(first, second, pool, slots, stacked):
    columns = [
        jnp.concatenate([pool[slots[j, target]] for j in range(slots.shape[0])], 0) for target in (first, second)
    ]
    return jnp.dot(stacked[...], jnp.concatenate(columns, 1), preferred_element_type=jnp.float32)


def upward_kernel(
    n,
    charges_hbm,
    basis_hbm,
    transfer_hbm,
    leaf_sends,
    parent_sends,
    leaf_sources,
    leaf_counts,
    parent_sources,
    parent_counts,
    leaf_coupling,
    parent_coupling,
    far_out,
    field_out,
    list_out,
    charges,
    basis_in,
    transfer,
    up_all,
    near,
    far_stage,
    fast_stage,
    parent_all,
    parent_stage,
    parent_pool,
    down,
    field,
    stacked,
    pstacked,
    zeros,
    near_vector,
    parent_vector,
    near_slots,
    parent_slots,
    load_sem,
    far_sem,
    fast_sem,
    parent_send_sem,
    parent_recv_sem,
    zero_sem,
    field_sem,
    slot_sem,
):
    me = lax.axis_index("leaf")
    odd = lax.rem(me, 2)
    fast_target = me + 1 - 2 * odd
    far_target = me - 1 + 2 * odd
    has_far = jnp.logical_and(far_target >= 0, far_target < n)
    leaves, rank, rhs = up_all.shape
    parents = parent_all.shape[0]
    side = far_stage.shape[0]
    piece = side // CHUNKS
    part = leaves // LOADS
    bf16 = up_all.dtype

    loads = [pltpu.make_async_copy(transfer_hbm, transfer, load_sem.at[2, 0])]
    for c in range(LOADS):
        rows = pl.ds(c * part, part)
        loads.append(pltpu.make_async_copy(basis_hbm.at[rows], basis_in.at[rows], load_sem.at[0, c]))
        loads.append(pltpu.make_async_copy(charges_hbm.at[rows], charges.at[rows], load_sem.at[1, c]))
    for load in loads[1:] + loads[:1]:
        load.start()

    barrier = pltpu.get_barrier_semaphore()

    def greet(k, carry):
        pl.semaphore_signal(barrier, inc=1, device_id=(lax.rem(me + k, n),), device_id_type=MESH)
        return carry

    lax.fori_loop(1, n, greet, 0)
    early = EARLY * piece
    spare = leaves + side + early
    near[spare] = jnp.zeros((rank, rhs), bf16)
    parent_pool[parents + n] = jnp.zeros((rank, rhs), bf16)
    zeros[...] = jnp.zeros_like(zeros)
    for j in range(leaf_coupling.shape[0]):
        stacked[:, j * rank : (j + 1) * rank] = leaf_coupling[j]
    for j in range(parent_coupling.shape[0]):
        pstacked[:, j * rank : (j + 1) * rank] = parent_coupling[j]
    width = leaf_sources.shape[0]
    limit = leaf_counts[...]
    codes, used = [], []
    for j in range(width):
        source = leaf_sources[j : j + 1, :]
        valid = limit > j
        fast_row = source - (leaves + (1 - odd) * side)
        far_row = source - (leaves + odd * side)
        row = jnp.where(
            source < leaves,
            source,
            jnp.where(
                jnp.logical_and(fast_row >= 0, fast_row < side),
                leaves + fast_row,
                jnp.where(jnp.logical_and(far_row >= 0, far_row < early), leaves + side + far_row, spare),
            ),
        )
        near_vector[j : j + 1, :] = jnp.where(valid, row, spare)
        codes.append(j * CODE + far_row - early)
        used.append(jnp.logical_and(valid, jnp.logical_and(far_row >= early, far_row < side)))
    parent_vector[...] = jnp.zeros_like(parent_vector)
    parent_limit = parent_counts[...]
    for j in range(parent_sources.shape[0]):
        parent_vector[j : j + 1, 0:parents] = jnp.where(parent_limit > j, parent_sources[j : j + 1, :], parents + n)
    slot_copies = [
        pltpu.make_async_copy(near_vector, near_slots, slot_sem.at[0]),
        pltpu.make_async_copy(parent_vector, parent_slots, slot_sem.at[1]),
    ]
    for copy in slot_copies:
        copy.start()

    place = jnp.zeros_like(limit)
    places = []
    for j in range(width):
        places.append(place)
        place = place + used[j].astype(jnp.int32)
    for p in range(width):
        entry = jnp.full_like(place, side - early)
        for j in range(p, width):
            entry = jnp.where(jnp.logical_and(used[j], places[j] == p), codes[j], entry)
        list_out[p : p + 1, :] = entry
    list_out[width : width + 1, :] = place
    for copy in slot_copies:
        copy.wait()
    for load in loads[1:]:
        load.wait()
    pl.semaphore_wait(barrier, n - 1)

    def up(first, second):
        both = jnp.dot(
            jnp.concatenate([basis_in[first], basis_in[second]], 0),
            jnp.concatenate([charges[first], charges[second]], 1),
            preferred_element_type=jnp.float32,
        )
        return both[:rank, :rhs].astype(bf16), both[rank:, rhs:].astype(bf16)

    def landing(c):
        if c < EARLY:
            return near.at[pl.ds(leaves + side + c * piece, piece)]
        return far_out.at[pl.ds((c - EARLY) * piece, piece)]

    def far_copy(c):
        rows = pl.ds(c * piece, piece)
        return pltpu.make_async_remote_copy(
            src_ref=far_stage.at[rows],
            dst_ref=landing(c),
            send_sem=far_sem.at[0, c],
            recv_sem=far_sem.at[1, c],
            device_id=(far_target,),
            device_id_type=MESH,
        )

    def zero_copy(c):
        return pltpu.make_async_copy(zeros, landing(c), zero_sem.at[c])

    def send_far(c, value):
        def fill_far(i, carry):
            at = c * piece + 2 * i
            far_stage[at], far_stage[at + 1] = value(leaf_sends[me, odd, at], leaf_sends[me, odd, at + 1])
            return carry

        lax.fori_loop(0, piece // 2, fill_far, 0, unroll=4)

        @pl.when(has_far)
        def _():
            far_copy(c).start()

        @pl.when(jnp.logical_not(has_far))
        def _():
            zero_copy(c).start()

    for c in range(EARLY):
        send_far(c, up)

    def up_rows(i, carry):
        for leaf, row in zip((2 * i, 2 * i + 1), up(2 * i, 2 * i + 1)):
            up_all[leaf] = row
            near[leaf] = row
        return carry

    lax.fori_loop(0, leaves // 2, up_rows, 0, unroll=4)
    def fill_fast(i, carry):
        fast_stage[i] = up_all[leaf_sends[me, 1 - odd, i]]
        return carry

    lax.fori_loop(0, side, fill_fast, 0, unroll=4)
    fast_copy = pltpu.make_async_remote_copy(
        src_ref=fast_stage,
        dst_ref=near.at[pl.ds(leaves, side)],
        send_sem=fast_sem.at[0],
        recv_sem=fast_sem.at[1],
        device_id=(fast_target,),
        device_id_type=MESH,
    )
    fast_copy.start()

    loads[0].wait()

    def up_parent(p, carry):
        row = lax.dot_general(
            transfer[p].reshape(8 * rank, rank),
            up_all[pl.ds(8 * p, 8)].reshape(8 * rank, rhs),
            CONTRACT_FIRST,
            preferred_element_type=jnp.float32,
        ).astype(bf16)
        parent_all[p] = row
        parent_pool[p] = row
        return carry

    lax.fori_loop(0, parents, up_parent, 0, unroll=2)

    def fill_parent(d, carry):
        parent_stage[d] = parent_all[parent_sends[me, d]]
        return carry

    lax.fori_loop(0, n, fill_parent, 0)

    def parent_copy(k):
        target = lax.rem(me + k, n)
        return pltpu.make_async_remote_copy(
            src_ref=parent_stage.at[target],
            dst_ref=parent_pool.at[parents + me],
            send_sem=parent_send_sem.at[k],
            recv_sem=parent_recv_sem.at[k],
            device_id=(target,),
            device_id_type=MESH,
        )

    def start_parent(k, carry):
        parent_copy(k).start()
        return carry

    lax.fori_loop(1, n, start_parent, 0)
    parent_pool[parents + me] = parent_stage[me]

    for c in range(EARLY, CHUNKS):
        send_far(c, lambda first, second: (up_all[first], up_all[second]))
    fast_copy.wait()
    for c in range(EARLY):

        @pl.when(has_far)
        def _():
            far_copy(c).wait_recv()

        @pl.when(jnp.logical_not(has_far))
        def _():
            zero_copy(c).wait()


    def near_pair(i, carry):
        pair = field_pair(2 * i, 2 * i + 1, near, near_slots, stacked)
        field[2 * i] = pair[:, :rhs]
        field[2 * i + 1] = pair[:, rhs:]
        return carry

    lax.fori_loop(0, leaves // 2, near_pair, 0, unroll=2)

    def wait_parent(k, carry):
        source = lax.rem(me - k + n, n)
        copy = pltpu.make_async_remote_copy(
            src_ref=parent_stage.at[lax.rem(me + k, n)],
            dst_ref=parent_pool.at[parents + source],
            send_sem=parent_send_sem.at[k],
            recv_sem=parent_recv_sem.at[k],
            device_id=(lax.rem(me + k, n),),
            device_id_type=MESH,
        )
        copy.wait_send()
        copy.wait_recv()
        return carry

    lax.fori_loop(1, n, wait_parent, 0)

    def parent_pair(i, carry):
        pair = field_pair(2 * i, 2 * i + 1, parent_pool, parent_slots, pstacked)
        down[2 * i] = pair[:, :rhs].astype(bf16)
        down[2 * i + 1] = pair[:, rhs:].astype(bf16)
        return carry

    lax.fori_loop(0, parents // 2, parent_pair, 0)

    def field_copy(c):
        rows = pl.ds(c * part, part)
        return pltpu.make_async_copy(field.at[rows], field_out.at[rows], field_sem.at[c])

    for c in range(LOADS):

        def push(i, carry):
            p = c * (parents // LOADS) + i
            pushed = jnp.dot(transfer[p].reshape(8 * rank, rank), down[p], preferred_element_type=jnp.float32)
            rows = pl.ds(8 * p, 8)
            field[rows] = field[rows] + pushed.reshape(8, rank, rhs)
            return carry

        lax.fori_loop(0, parents // LOADS, push, 0, unroll=2)
        field_copy(c).start()
    for c in range(LOADS):
        field_copy(c).wait()
    for c in range(CHUNKS):

        @pl.when(has_far)
        def _():
            far_copy(c).wait_send()

    for c in range(EARLY, CHUNKS):

        @pl.when(has_far)
        def _():
            far_copy(c).wait_recv()

        @pl.when(jnp.logical_not(has_far))
        def _():
            zero_copy(c).wait()


def downward_kernel(lists, leaf_coupling, far, field, basis_out, potential, pool, even_side, odd_side, total, sem):
    step = pl.program_id(0)
    block, rank, rhs = total.shape
    side = far.shape[0]
    width = leaf_coupling.shape[0]

    @pl.when(step == 0)
    def _():
        copy = pltpu.make_async_copy(far, pool.at[pl.ds(0, side)], sem)
        copy.start()
        pool[side] = jnp.zeros((rank, rhs), pool.dtype)
        blank = jnp.zeros((rank, rank), pool.dtype)
        for j in range(width):
            even_side[j] = jnp.concatenate([leaf_coupling[j], blank], 1)
            odd_side[j] = jnp.concatenate([blank, leaf_coupling[j]], 1)
        copy.wait()

    def group(targets, g):
        left, right = [], []
        for target in targets:
            codes = [lists[GROUP * g + k, target] for k in range(GROUP)]
            slot = [lax.shift_right_logical(code, 10) for code in codes]
            sides = [even_side[slot[k]] + odd_side[slot[k + 1]] for k in range(0, GROUP, 2)]
            left.append(jnp.concatenate(sides, 1))
            right.append(jnp.concatenate([pool[jnp.bitwise_and(code, CODE - 1)] for code in codes], 0))
        product = jnp.dot(
            jnp.concatenate(left, 0), jnp.concatenate(right, 1), preferred_element_type=jnp.float32
        )
        return [product[k * rank : (k + 1) * rank, k * rhs : (k + 1) * rhs] for k in range(len(targets))]

    for leaf in range(0, block, 2):
        target = step * block + leaf
        first, second = group((target, target + 1), 0)
        total[leaf] = field[leaf] + first
        total[leaf + 1] = field[leaf + 1] + second

    def rest(leaf):
        target = step * block + leaf
        count = lists[width, target]

        @pl.when(count > GROUP)
        def _():
            def more(g, carry):
                total[leaf] += group((target,), g)[0]
                return carry

            lax.fori_loop(1, lax.shift_right_logical(count + (GROUP - 1), 2), more, 0)

    for leaf in range(block):
        rest(leaf)
    blank = jnp.zeros((rank, rhs), jnp.bfloat16)
    for leaf in range(0, block, 2):
        first, second = (total[leaf + k].astype(jnp.bfloat16) for k in range(2))
        diagonal = jnp.concatenate(
            [jnp.concatenate([first, blank], 1), jnp.concatenate([blank, second], 1)], 0
        )
        both = lax.dot_general(
            basis_out[leaf : leaf + 2].reshape(2 * rank, basis_out.shape[2]),
            diagonal,
            CONTRACT_FIRST,
            preferred_element_type=jnp.float32,
        ).astype(potential.dtype)
        potential[leaf] = both[:, :rhs]
        potential[leaf + 1] = both[:, rhs:]


def shards(
    n,
    charges,
    basis_in,
    basis_out,
    transfer,
    leaf_coupling,
    parent_coupling,
    leaf_sources,
    leaf_counts,
    leaf_sends,
    parent_sources,
    parent_counts,
    parent_sends,
):
    leaves, points, rhs = charges.shape
    rank = basis_in.shape[1]
    parents = transfer.shape[0]
    side = leaf_sends.shape[2]
    width = leaf_sources.shape[1]
    pwidth = parent_sources.shape[1]
    block = 32
    bf16 = jnp.bfloat16
    list_rows = width + 8
    early = EARLY * (side // CHUNKS)
    far, field, lists = pl.pallas_call(
        functools.partial(upward_kernel, n),
        out_shape=(
            jax.ShapeDtypeStruct((side - early, rank, rhs), bf16),
            jax.ShapeDtypeStruct((leaves, rank, rhs), jnp.float32),
            jax.ShapeDtypeStruct((list_rows, leaves), jnp.int32),
        ),
        in_specs=[ANY, ANY, ANY, SMEM, SMEM] + [VMEM] * 6,
        out_specs=(ANY, ANY, VMEM),
        scratch_shapes=[
            pltpu.VMEM((leaves, points, rhs), bf16),
            pltpu.VMEM((leaves, rank, points), bf16),
            pltpu.VMEM((parents, 8, rank, rank), bf16),
            pltpu.VMEM((leaves, rank, rhs), bf16),
            pltpu.VMEM((leaves + side + early + 1, rank, rhs), bf16),
            pltpu.VMEM((side, rank, rhs), bf16),
            pltpu.VMEM((side, rank, rhs), bf16),
            pltpu.VMEM((parents, rank, rhs), bf16),
            pltpu.VMEM((n, rank, rhs), bf16),
            pltpu.VMEM((parents + n + 1, rank, rhs), bf16),
            pltpu.VMEM((parents, rank, rhs), bf16),
            pltpu.VMEM((leaves, rank, rhs), jnp.float32),
            pltpu.VMEM((rank, width * rank), bf16),
            pltpu.VMEM((rank, pwidth * rank), bf16),
            pltpu.VMEM((side // CHUNKS, rank, rhs), bf16),
            pltpu.VMEM((width, leaves), jnp.int32),
            pltpu.VMEM((pwidth, -(-parents // 128) * 128), jnp.int32),
            pltpu.SMEM((width, leaves), jnp.int32),
            pltpu.SMEM((pwidth, -(-parents // 128) * 128), jnp.int32),
            pltpu.SemaphoreType.DMA((3, LOADS)),
            pltpu.SemaphoreType.DMA((2, CHUNKS)),
            pltpu.SemaphoreType.DMA((2,)),
            pltpu.SemaphoreType.DMA((n,)),
            pltpu.SemaphoreType.DMA((n,)),
            pltpu.SemaphoreType.DMA((CHUNKS,)),
            pltpu.SemaphoreType.DMA((LOADS,)),
            pltpu.SemaphoreType.DMA((2,)),
        ],
        compiler_params=pltpu.CompilerParams(
            collective_id=0, has_side_effects=True, vmem_limit_bytes=56 * 2**20
        ),
        name="upward",
    )(
        charges,
        basis_in,
        transfer,
        leaf_sends,
        parent_sends,
        leaf_sources.T,
        leaf_counts[None, :],
        parent_sources.T,
        parent_counts[None, :],
        leaf_coupling,
        parent_coupling,
    )
    return pl.pallas_call(
        downward_kernel,
        out_shape=jax.ShapeDtypeStruct((leaves, points, rhs), bf16),
        grid_spec=pltpu.PrefetchScalarGridSpec(
            num_scalar_prefetch=1,
            grid=(leaves // block,),
            in_specs=[
                pl.BlockSpec(leaf_coupling.shape, lambda i, *_: (0, 0, 0)),
                ANY,
                pl.BlockSpec((block, rank, rhs), lambda i, *_: (i, 0, 0)),
                pl.BlockSpec((block, rank, points), lambda i, *_: (i, 0, 0)),
            ],
            out_specs=pl.BlockSpec((block, points, rhs), lambda i, *_: (i, 0, 0)),
            scratch_shapes=[
                pltpu.VMEM((side - early + 1, rank, rhs), bf16),
                pltpu.VMEM((width, rank, 2 * rank), bf16),
                pltpu.VMEM((width, rank, 2 * rank), bf16),
                pltpu.VMEM((block, rank, rhs), jnp.float32),
                pltpu.SemaphoreType.DMA,
            ],
        ),
        compiler_params=pltpu.CompilerParams(vmem_limit_bytes=60 * 2**20),
        name="downward",
    )(lists, leaf_coupling, far, field, basis_out)


def solution(mesh):
    return jax.shard_map(
        functools.partial(shards, mesh.shape["leaf"]),
        mesh=mesh,
        in_specs=(
            P("leaf", None, None),
            P("leaf", None, None),
            P("leaf", None, None),
            P("leaf", None, None, None),
            P(),
            P(),
            P("leaf", None),
            P("leaf"),
            P(),
            P("leaf", None),
            P("leaf"),
            P(),
        ),
        out_specs=P("leaf", None, None),
        check_vma=False,
    )
```
